32 devices in a mesh: dom: 2 (over y), feat: 4 (over z), dp: 4 (over x, core).
Axes of the slice: x: 2, y: 2, z: 4, core: 2. Of those that a mesh axis runs over, the one named last changes fastest.
Arguments:
- layer_in: bfloat16 [32768, 2048], P(('dom', 'dp', 'feat')), parts along dimension 0, may hold values from -6 to 6
- grad_out: bfloat16 [32768, 2048], P(('dom', 'dp', 'feat')), parts along dimension 0, may hold values from -6 to 6
- in_proj: bfloat16 [2048, 256], replicated, may hold values from -0.125 to 0.125
- out_proj: bfloat16 [2048, 256], replicated, may hold values from -0.125 to 0.125
- queries: bfloat16 [2048, 65536], P(('dom', 'dp'), 'feat'), parts along dimension 0, may hold values from -0.00390625 to 0.00390625
- seq_ids: int32 [32, 1024], P(('dom', 'dp', 'feat')), parts along dimension 0, may hold values from 0 to 15, never falling along the last dimension, each value on 1 to 128 neighbouring positions
- valid_counts: int32 [512], P(('dom', 'dp', 'feat')), parts along dimension 0, may hold values from 16 to 128
- owner_order: int32 [2048], P(('dom', 'dp')), parts along dimension 0, may hold values from 0 to 1023, as said below
Outputs:
- scores: float32 [2048, 256], P(('dom', 'dp', 'feat')), parts along dimension 0
The draws below stay inside these ranges and needn't reach their ends.
There are 2 independent parts, one for each index of `dom`. The reference program is written for one: setup_inputs(seed, part) draws one part's arguments, and reference() takes and returns one part's arrays. A program takes and returns all parts, laid end to end along the dimension named above; an argument that names none is the same for every part. Nothing has to cross between parts.
Inputs may be any that keep to these rules, and one draw needn't show every extreme that they name: `seq_ids`: each row numbers the 16 sequences of one block in order, never falling; every number appears. `owner_order`: within each aligned block of 256 rows, a permutation of that block's row numbers.
All inputs are finite; a program needn't handle non-finite values.
Results may differ from the reference program's by a relative error of at most 0.005.
Values may be sent and summed in bfloat16 or wider, within the bound.
No kernel may reach another device: no remote copies, remote signals or barrier semaphores. Data moves between devices by JAX's collectives and lax.ppermute only.
A program may use at most 64 MiB of HBM per device.

```python
import math
import jax
import jax.numpy as jnp
import numpy as np
from jax import lax

D = 2048
R = 256
FEATS = 65536
SEQ_DEV = 16
SEQ_LEN = 64
WIN = 128
TOK_DEV = 1024
GROUPS = 16
TOKENS = 16384
SEQUENCES = 256
Q_DP = 256
QUERIES = 1024


def draw_owner_order(key, part):
    blocks = QUERIES // Q_DP
    subkeys = jax.random.split(jax.random.fold_in(key, 17), blocks)

    def one_order(subkey):
        return jax.random.permutation(subkey, Q_DP).astype(jnp.int32)
    orders = jax.vmap(one_order)(subkeys)
    offsets = (jnp.arange(blocks, dtype=jnp.int32) * Q_DP)[:, None]
    return (orders + offsets).reshape(QUERIES).astype(jnp.int32)


def plant(drawn, rng, least, top_value):
    place = [jax.random.randint(jax.random.fold_in(rng, axis), (), 0, length) for axis, length in enumerate(drawn.shape)]
    longest = drawn.shape.index(max(drawn.shape))
    neighbour = place[:longest] + [(place[longest] + 1) % drawn.shape[longest]] + place[longest + 1:]
    return drawn.at[tuple(place)].set(least).at[tuple(neighbour)].set(top_value)


def strengthened(entries, own_key, source, target, shards_of, factor):
    owner, partner = [(jnp.arange(entries.shape[axis_at]) // (entries.shape[axis_at] // shards_of)).reshape([-1 if axis == axis_at else 1 for axis in range(entries.ndim)]) for axis_at in (source, target)]
    chosen = jax.random.permutation(own_key, shards_of)[partner]
    strong = (owner == chosen) | (owner == (partner + shards_of // 2) % shards_of)
    return jnp.where(strong, factor * entries, entries)


def block_levels(key, extent, pieces, least, largest):
    def one(dim, shards_of):
        heights = jax.random.uniform(jax.random.fold_in(jax.random.fold_in(key, 6), dim), (shards_of,), jnp.float32, least / len(pieces), largest / len(pieces))
        return jnp.repeat(jnp.exp(heights), extent[dim] // shards_of).reshape((-1,) + (1,) * (len(extent) - dim - 1))

    level = one(*pieces[0])
    for cut in pieces[1:]:
        level = level * one(*cut)
    return level


def split_up(count, total, bound, lean):
    loads = [(1 << 20) // math.isqrt(standing ** lean) + 1 for standing in range(2, count + 1)]
    spare, given = total - bound - (count - 1), [1] * (count - 1)
    while spare > 0:
        free = [i for i in range(count - 1) if given[i] < bound]
        mass, left = sum([loads[i] for i in free]), spare
        for i in free:
            more = min(bound - given[i], max(1, left * loads[i] // mass), spare)
            given[i] = given[i] + more
            spare = spare - more
    return np.array([bound] + given)


def uneven(rng, count, total, reach, skew):
    if count == 2:
        one = jax.random.randint(rng, (), max(1, total - reach), min(reach, total - 1) + 1)
        return jnp.stack([one, total - one])
    lengths = jnp.asarray(split_up(count, total, reach, skew), jnp.int32)
    couples = (count - 1) // 2
    source_of, receiver = lengths[1:1 + 2 * couples:2], lengths[2:2 + 2 * couples:2]
    slack = jnp.minimum(source_of - 1, reach - receiver)
    passed = jax.random.randint(jax.random.fold_in(rng, 1), (couples,), 0, 1 << 20) % (slack + 1)
    lengths = lengths.at[1:1 + 2 * couples:2].set(source_of - passed).at[2:2 + 2 * couples:2].set(receiver + passed)
    return lengths[jax.random.permutation(jax.random.fold_in(rng, 2), count)]


def scatter_about(key, extent, width, limit, cuts=(), kind=jnp.bfloat16):
    values = width * jax.random.normal(key, extent, jnp.float32)
    if cuts:
        values = values * block_levels(key, extent, cuts, -0.22, 0.18)
    return jnp.clip(values, -limit, limit).astype(kind)


def bell_draw_with(key, dims, deviation, reach, pieces, heavy, held_as=jnp.bfloat16):
    entries = deviation * jax.random.normal(key, dims, jnp.float32)
    if pieces:
        entries = entries * block_levels(key, dims, pieces, -0.22, 0.18)
    return jnp.clip(strengthened(entries, jax.random.fold_in(key, 3), *heavy), -reach, reach).astype(held_as)


def setup_inputs(seed: int = 0, part: int = 0) -> dict:
    splits = jax.random.split(jax.random.key(seed), 9)
    own_keys = jax.random.split(jax.random.fold_in(splits[8], part), 9)
    return {
        "layer_in": scatter_about(own_keys[0], (TOKENS, D), 1.0, 6.0, ((0, 16),)),
        "grad_out": scatter_about(own_keys[1], (TOKENS, D), 1.0, 6.0, ((0, 16),)),
        "in_proj": scatter_about(splits[2], (D, R), D ** -0.5, 0.125),
        "out_proj": scatter_about(splits[3], (D, R), D ** -0.5, 0.125),
        "queries": bell_draw_with(own_keys[4], (QUERIES, FEATS), (FEATS * SEQ_LEN) ** -0.5, 0.00390625, ((0, 4), (1, 4)), (1, 0, 4, 2.0)),
        "seq_ids": jax.vmap(lambda own: jnp.searchsorted(jnp.cumsum(uneven(own, SEQ_DEV, TOK_DEV, WIN, 0)), jnp.arange(TOK_DEV), side="right"))(jax.random.split(own_keys[5], GROUPS)).reshape((GROUPS, TOK_DEV)).astype(jnp.int32),
        "valid_counts": plant(jax.random.randint(own_keys[6], (SEQUENCES,), WIN // 8, WIN + 1), jax.random.fold_in(own_keys[6], 1), WIN // 8, WIN).astype(jnp.int32),
        "owner_order": draw_owner_order(jax.random.fold_in(jax.random.fold_in(splits[8], part), 71), part),
    }


def sequence_grads(in_low, out_low, labels, counts):
    member = (labels[:, None] == jnp.arange(SEQ_DEV, dtype=jnp.int32)[None, :]).astype(jnp.int32)
    seg_len = jnp.sum(member, axis=0).astype(jnp.int32)
    starts = (jnp.cumsum(seg_len) - seg_len).astype(jnp.int32)
    position = jnp.arange(TOK_DEV, dtype=jnp.int32) - starts[labels]
    counted = (position < counts[labels]).astype(jnp.float32)
    weighted = in_low.astype(jnp.float32) * counted[:, None]
    member_f = member.astype(jnp.float32)
    grads = jnp.einsum("ts,ti,tj->sij", member_f, weighted, out_low.astype(jnp.float32), precision=lax.Precision.HIGHEST)
    return grads.reshape(SEQ_DEV, R * R).astype(jnp.bfloat16)


def reference(layer_in, grad_out, in_proj, out_proj, queries, seq_ids, valid_counts, owner_order):
    layer_blocks = layer_in.reshape(GROUPS, TOK_DEV, D)
    grad_blocks = grad_out.reshape(GROUPS, TOK_DEV, D)
    count_blocks = valid_counts.reshape(GROUPS, SEQ_DEV)

    def one_block(inputs):
        layer_rows, grad_rows, labels, counts = inputs
        in_low = jnp.dot(layer_rows, in_proj, preferred_element_type=jnp.float32).astype(jnp.bfloat16)
        out_low = jnp.dot(grad_rows, out_proj, preferred_element_type=jnp.float32).astype(jnp.bfloat16)
        return sequence_grads(in_low, out_low, labels, counts)

    seq_grads = lax.map(one_block, (layer_blocks, grad_blocks, seq_ids, count_blocks))
    seq_grads = seq_grads.reshape(SEQUENCES, R * R)
    score = lax.dot_general(queries, seq_grads, (((1,), (1,)), ((), ())), preferred_element_type=jnp.float32)
    return jnp.take(score, owner_order, axis=0)
```

```python
import functools

import jax
import jax.numpy as jnp
from jax import lax
from jax.experimental import pallas as pl
from jax.experimental.pallas import tpu as pltpu
from jax.sharding import PartitionSpec as P

F32 = jnp.float32
BF16 = jnp.bfloat16
NT = (((1,), (1,)), ((), ()))
MIB = 1 << 20
TOKEN_BLOCK = 256
ROW_BLOCK = 16
TURN_BLOCK = 2048
FREE = pl.CostEstimate(flops=0, bytes_accessed=0, transcendentals=0)
IN_HBM = pl.BlockSpec(memory_space=pltpu.HBM)
IN_VMEM = pl.BlockSpec(memory_space=pltpu.VMEM)
PARAMS = pltpu.CompilerParams(vmem_limit_bytes=16 * MIB)


def hbm(array):
    return pltpu.with_memory_space_constraint(array, pltpu.HBM)


def counted_mask(ids, valid):
    seqs, tokens = valid.shape[1], ids.shape[1]
    eye = lax.broadcasted_iota(jnp.int32, (seqs, seqs), 0) == lax.broadcasted_iota(jnp.int32, (seqs, seqs), 1)
    limit = jnp.sum(jnp.where(eye, jnp.broadcast_to(valid, (seqs, seqs)), 0), axis=1, keepdims=True)
    ids = jnp.broadcast_to(ids, (seqs, tokens))
    seq = lax.broadcasted_iota(jnp.int32, (seqs, tokens), 0)
    start = jnp.sum((ids < seq).astype(jnp.int32), axis=1, keepdims=True)
    position = lax.broadcasted_iota(jnp.int32, (seqs, tokens), 1) - start
    return jnp.where((ids == seq) & (position < limit), 1.0, 0.0).astype(F32)


def grads_kernel(parts, ask, layer, grad, in_proj, out_proj, ids, valid, *rest):
    outs = rest[: len(ask)]
    layer_v, grad_v, in_v, out_v, ids_v, valid_v, in_t, out_low, mask, sems = rest[len(ask):]
    tokens = layer.shape[0]
    block = min(TOKEN_BLOCK, tokens)
    spans = [pl.ds(t, block) for t in range(0, tokens, block)]
    copies = []

    def fetch(source, target):
        copy = pltpu.make_async_copy(source, target, sems.at[len(copies)])
        copy.start()
        copies.append(copy)
        return copy

    out_copy = fetch(out_proj, out_v)
    grad_copies = [fetch(grad.at[spans[0]], grad_v.at[spans[0]])]
    small_copies = [fetch(ids, ids_v), fetch(valid, valid_v)]
    grad_copies += [fetch(grad.at[s], grad_v.at[s]) for s in spans[1:]]
    in_copy = fetch(in_proj, in_v)
    layer_copies = [fetch(layer.at[s], layer_v.at[s]) for s in spans]
    for copy in small_copies:
        copy.wait()
    mask[...] = counted_mask(ids_v[...], valid_v[...])
    out_copy.wait()
    for s, copy in zip(spans, grad_copies):
        copy.wait()
        out_low[s, :] = jnp.dot(grad_v[s, :], out_v[...], preferred_element_type=F32).astype(BF16)
    in_copy.wait()
    for s, copy in zip(spans, layer_copies):
        copy.wait()
        low = jnp.dot(layer_v[s, :], in_v[...], preferred_element_type=F32).astype(BF16)
        in_t[:, s] = low.astype(F32).T
    width = in_t.shape[0]
    seqs = mask.shape[0]
    span = width // parts
    me = lax.axis_index("feat")
    for (k, piece, pieces), out in zip(ask, outs):
        size = span // pieces
        small = min(ROW_BLOCK, size)
        base = pl.multiple_of((me ^ k) * span + piece * size, size)
        for r in range(0, size, small):
            rows = in_t[pl.ds(base + r, small), :]
            left = (rows[:, None, :] * mask[...][None]).astype(BF16).reshape(small * seqs, tokens)
            got = jnp.dot(left, out_low[...], preferred_element_type=F32).astype(BF16)
            out[pl.ds(r, small)] = got.reshape(small, seqs, got.shape[1])


def grads(parts, ask, layer_in, grad_out, in_proj, out_proj, seq_ids, valid_counts):
    tokens, model = layer_in.shape
    width = in_proj.shape[1]
    seqs = valid_counts.shape[0]
    block = min(TOKEN_BLOCK, tokens)
    args = (layer_in, grad_out, in_proj, out_proj, seq_ids, valid_counts.reshape(1, seqs))
    return pl.pallas_call(
        functools.partial(grads_kernel, parts, ask),
        in_specs=[IN_HBM] * 6,
        out_specs=[IN_VMEM] * len(ask),
        out_shape=[pltpu.VMEM((width // parts // part[2], seqs, width), BF16) for part in ask],
        scratch_shapes=[
            pltpu.VMEM((tokens, model), BF16),
            pltpu.VMEM((tokens, model), BF16),
            pltpu.VMEM((model, width), BF16),
            pltpu.VMEM((model, width), BF16),
            pltpu.VMEM((1, tokens), jnp.int32),
            pltpu.VMEM((1, seqs), jnp.int32),
            pltpu.VMEM((width, tokens), F32),
            pltpu.VMEM((tokens, width), BF16),
            pltpu.VMEM((seqs, tokens), F32),
            pltpu.SemaphoreType.DMA((4 + 2 * (tokens // block),)),
        ],
        compiler_params=PARAMS,
        cost_estimate=FREE,
        name="sequence_grads",
    )(*map(hbm, args))


def turn_kernel(source, out, held, sems):
    depth = source.shape[1]
    block = min(TURN_BLOCK, depth)
    copies = []
    for n, start in enumerate(range(0, depth, block)):
        span = pl.ds(start, block)
        copies.append(pltpu.make_async_copy(source.at[:, span], held.at[:, span], sems.at[n]))
        copies[-1].start()
    for n, start in enumerate(range(0, depth, block)):
        copies[n].wait()
        span = pl.ds(start, block)
        out[span, :] = held[:, span].T


def turn(queries):
    rows, depth = queries.shape
    return pl.pallas_call(
        turn_kernel,
        in_specs=[IN_HBM],
        out_specs=IN_VMEM,
        out_shape=pltpu.VMEM((depth, rows), BF16),
        scratch_shapes=[pltpu.VMEM((rows, depth), BF16), pltpu.SemaphoreType.DMA((-(-depth // TURN_BLOCK),))],
        compiler_params=PARAMS,
        cost_estimate=FREE,
        name="turn",
    )(hbm(queries))


def score_kernel(offset, count, first, last, *rest):
    rest = list(rest)
    queries = [rest.pop(0), rest.pop(0)]
    pieces = [rest.pop(0) for _ in range(count)]
    totals = [None, None] if first else [rest[0][0], rest.pop(0)[1]]
    orders = [rest.pop(0), rest.pop(0)] if last else None
    outs = rest
    depth, _, width = pieces[0].shape
    for i in range(depth):
        left = jnp.concatenate([piece[i] for piece in pieces], axis=0)
        for n in range(2):
            right = queries[n][(offset + i) * width:(offset + i + 1) * width, :]
            got = jnp.dot(left, right, preferred_element_type=F32)
            totals[n] = got if totals[n] is None else totals[n] + got
    if not last:
        for n in range(2):
            outs[0][n] = totals[n]
        return
    cols, q_rows = totals[0].shape
    rows = q_rows // len(outs)
    for n in range(2):
        high = totals[n].astype(BF16)
        left = totals[n] - high.astype(F32)
        middle = left.astype(BF16)
        low = (left - middle.astype(F32)).astype(BF16)
        wanted = lax.rem(orders[n][...], q_rows)
        pick = (lax.broadcasted_iota(jnp.int32, (q_rows, q_rows), 0) == wanted).astype(F32).astype(BF16)
        picked = jnp.dot(jnp.concatenate([high, middle, low], axis=0), pick, preferred_element_type=F32)
        picked = picked[:cols] + (picked[cols:2 * cols] + picked[2 * cols:])
        for m, out in enumerate(outs):
            out[:, n * rows:(n + 1) * rows] = picked[:, m * rows:(m + 1) * rows]


def score(parts, queries, offset, pieces, before=None, orders=None):
    _, seqs, width = pieces[0].shape
    q_rows = queries[0].shape[1]
    cols = len(pieces) * seqs
    args = [*queries, *pieces]
    if before is not None:
        args.append(before)
    if orders is None:
        shapes = [jax.ShapeDtypeStruct((2, cols, q_rows), F32)]
    else:
        args += orders
        shapes = [jax.ShapeDtypeStruct((cols, 2 * q_rows // parts), F32)] * parts
    done = pl.pallas_call(
        functools.partial(score_kernel, offset, len(pieces), before is None, orders is not None),
        in_specs=[IN_VMEM] * len(args),
        out_specs=[IN_VMEM] * len(shapes),
        out_shape=shapes,
        compiler_params=PARAMS,
        cost_estimate=FREE,
        name="score",
    )(*args)
    return done[0] if orders is None else done


def reduce_kernel(parts, crossing, seqs, sets, *refs):
    own, other = refs[-2:]
    rows = own.shape[1]
    where = {k: (g, n) for g, ks in enumerate(sets) for n, k in enumerate(ks)}
    size = crossing * seqs
    for k in range(parts):
        total = None
        for m in range(parts):
            g, n = where[k ^ m]
            got = refs[g * parts + m][pl.ds(n * size, size), :]
            total = got if total is None else total + got
        own[pl.ds(k * size, size), :] = total[:, :rows]
        other[pl.ds(k * size, size), :] = total[:, rows:]


def reduce(parts, crossing, seqs, sets, messages):
    flat = [message for group in messages for message in group]
    shape = jax.ShapeDtypeStruct((parts * crossing * seqs, flat[0].shape[1] // 2), F32)
    return pl.pallas_call(
        functools.partial(reduce_kernel, parts, crossing, seqs, sets),
        in_specs=[IN_VMEM] * len(flat),
        out_specs=[IN_VMEM] * 2,
        out_shape=[shape] * 2,
        compiler_params=PARAMS,
        cost_estimate=FREE,
        name="reduce",
    )(*flat)


def finish_kernel(parts, dp, seqs, own, other, out, columns):
    z, d = lax.axis_index("feat"), lax.axis_index("dp")
    crossed = (0, dp // 2)
    for k in range(parts):
        for n, e in enumerate(crossed):
            for flip, ref in ((0, own), (1, other)):
                place = ((d ^ e ^ flip) * parts + (z ^ k)) * seqs
                rows = ref[pl.ds((k * len(crossed) + n) * seqs, seqs), :]
                columns[pl.ds(pl.multiple_of(place, seqs), seqs), :] = rows
    out[...] = columns[...].T


def finish(parts, dp, seqs, own, other):
    rows = own.shape[1]
    total = parts * dp * seqs
    return pl.pallas_call(
        functools.partial(finish_kernel, parts, dp, seqs),
        in_specs=[IN_VMEM] * 2,
        out_specs=IN_VMEM,
        out_shape=jax.ShapeDtypeStruct((rows, total), F32),
        scratch_shapes=[pltpu.VMEM((total, rows), F32)],
        compiler_params=PARAMS,
        cost_estimate=FREE,
        name="finish",
    )(own, other)


def swap(array, axis, size, by):
    return lax.ppermute(array, axis, [(i, i ^ by) for i in range(size)])


def after(array, *earlier):
    return lax.optimization_barrier((array, *earlier))[0]


def direct(parts, dp, layer_in, grad_out, in_proj, out_proj, queries, seq_ids, valid_counts, owner_order):
    seqs = valid_counts.shape[0]
    half = in_proj.shape[1] // parts // 2
    me = lax.axis_index("feat")
    cross = lambda array: swap(array, "dp", dp, dp // 2)
    pair = lambda array: swap(array, "dp", dp, 1)
    move = lambda array, k: swap(array, "feat", parts, k)
    order = jnp.take(owner_order.reshape(parts, -1), me ^ jnp.arange(parts), axis=0).reshape(1, -1)
    orders = [order, pair(order)]
    ask = [(1, 0, 1), (2, 0, 2), (3, 0, 2), (0, 0, 1), (2, 1, 2), (3, 1, 2)]
    g1, g2a, g3a, g0, g2b, g3b = grads(parts, ask, layer_in, grad_out, in_proj, out_proj, seq_ids, valid_counts)
    turned = [turn(queries), turn(pair(queries))]
    x0 = cross(g0)
    z1, z2a, z3a = move(g1, 1), move(g2a, 2), move(g3a, 3)
    z2b, z3b = move(after(g2b, x0), 2), move(after(g3b, x0), 3)
    x1, x2a, x3a, x2b, x3b = map(cross, (z1, z2a, z3a, z2b, z3b))
    near = score(parts, turned, 0, [g0, x0, z1, x1], None, orders)
    part = score(parts, turned, 0, [z2a, x2a, z3a, x3a])
    far = score(parts, turned, half, [z2b, x2b, z3b, x3b], part, orders)
    messages = [[group[0]] + [move(group[m], m) for m in range(1, parts)] for group in (near, far)]
    own, other = reduce(parts, 2, seqs, [[0, 1], [2, 3]], messages)
    return finish(parts, dp, seqs, own, pair(other))


def gathered(parts, dp, layer_in, grad_out, in_proj, out_proj, queries, seq_ids, valid_counts, owner_order):
    ask = [(k, 0, 1) for k in range(parts)]
    own = jnp.stack(grads(parts, ask, layer_in, grad_out, in_proj, out_proj, seq_ids, valid_counts))
    own = jnp.take(own, lax.axis_index("feat") ^ jnp.arange(parts), axis=0)
    size = own.shape[1]
    rows = lax.all_to_all(own, "feat", split_axis=0, concat_axis=0, tiled=True)
    rows = lax.all_gather(rows, "dp", axis=0, tiled=True)
    q_rows = queries.shape[0]
    by_row = queries.reshape(q_rows, size, -1)
    scored = jnp.einsum("qij,gisj->qgs", by_row, rows, preferred_element_type=F32)
    scored = jnp.take(scored.reshape(q_rows, -1), owner_order % q_rows, axis=0)
    return lax.psum_scatter(scored, "feat", scatter_dimension=0, tiled=True)


def solution(mesh):
    parts, dp = mesh.shape["feat"], mesh.shape["dp"]
    in_specs = (
        P(("dom", "dp", "feat"), None),
        P(("dom", "dp", "feat"), None),
        P(),
        P(),
        P(("dom", "dp"), "feat"),
        P(("dom", "dp", "feat"), None),
        P(("dom", "dp", "feat")),
        P(("dom", "dp")),
    )
    out_specs = P(("dom", "dp", "feat"), None)
    body = functools.partial(direct if parts == 4 and dp == 4 else gathered, parts, dp)
    return jax.shard_map(body, mesh=mesh, in_specs=in_specs, out_specs=out_specs, check_vma=False)
```

```python
import functools
import math

import jax
import jax.numpy as jnp
from jax import lax
from jax.experimental import pallas as pl
from jax.experimental.pallas import tpu as pltpu
from jax.sharding import PartitionSpec as P

F32 = jnp.float32
BF16 = jnp.bfloat16
NT = (((1,), (1,)), ((), ()))
MIB = 1 << 20
TOKEN_BLOCK = 512
ROW_BLOCK = 16
QUERY_BLOCK = 8
SPLIT = 4
QUERY_SLOTS = 8
FREE = pl.CostEstimate(flops=0, bytes_accessed=0, transcendentals=0)
IN_HBM = pl.BlockSpec(memory_space=pltpu.HBM)
IN_VMEM = pl.BlockSpec(memory_space=pltpu.VMEM)
SMALL = pltpu.CompilerParams(vmem_limit_bytes=6 * MIB)
PARAMS = pltpu.CompilerParams(vmem_limit_bytes=16 * MIB)


def hbm(array):
    return pltpu.with_memory_space_constraint(array, pltpu.HBM)


def counted_mask(ids, valid):
    seqs, tokens = valid.shape[1], ids.shape[1]
    eye = lax.broadcasted_iota(jnp.int32, (seqs, seqs), 0) == lax.broadcasted_iota(jnp.int32, (seqs, seqs), 1)
    limit = jnp.sum(jnp.where(eye, jnp.broadcast_to(valid, (seqs, seqs)), 0), axis=1, keepdims=True)
    ids = jnp.broadcast_to(ids, (seqs, tokens))
    seq = lax.broadcasted_iota(jnp.int32, (seqs, tokens), 0)
    start = jnp.sum((ids < seq).astype(jnp.int32), axis=1, keepdims=True)
    position = lax.broadcasted_iota(jnp.int32, (seqs, tokens), 1) - start
    return jnp.where((ids == seq) & (position < limit), 1.0, 0.0).astype(F32)


def grads_kernel(parts, ask, layer, grad, in_proj, out_proj, ids, valid, *rest):
    outs = rest[: len(ask)]
    layer_v, grad_v, in_v, out_v, ids_v, valid_v, in_t, out_low, mask, sems = rest[len(ask):]
    tokens = layer.shape[0]
    block = min(TOKEN_BLOCK, tokens)
    spans = [pl.ds(t, block) for t in range(0, tokens, block)]
    copies = []

    def fetch(source, target, at):
        copy = pltpu.make_async_copy(source, target, sems.at[at])
        copy.start()
        copies.append(copy)
        return copy

    out_copy = fetch(out_proj, out_v, 0)
    grad_copies = [fetch(grad.at[spans[0]], grad_v.at[spans[0]], 4)]
    small_copies = [fetch(ids, ids_v, 1), fetch(valid, valid_v, 2)]
    grad_copies += [fetch(grad.at[s], grad_v.at[s], 5 + n) for n, s in enumerate(spans[1:])]
    in_copy = fetch(in_proj, in_v, 3)
    layer_copies = [fetch(layer.at[s], layer_v.at[s], 4 + len(spans) + n) for n, s in enumerate(spans)]
    for copy in small_copies:
        copy.wait()
    mask[...] = counted_mask(ids_v[...], valid_v[...])
    out_copy.wait()
    @pl.loop(0, len(spans))
    def _(n):
        s = pl.ds(pl.multiple_of(n * block, block), block)
        pltpu.make_async_copy(grad.at[s], grad_v.at[s], sems.at[4 + n]).wait()
        out_low[s, :] = jnp.dot(grad_v[s, :], out_v[...], preferred_element_type=F32).astype(BF16)
    in_copy.wait()
    @pl.loop(0, len(spans))
    def _(n):
        s = pl.ds(pl.multiple_of(n * block, block), block)
        pltpu.make_async_copy(layer.at[s], layer_v.at[s], sems.at[4 + len(spans) + n]).wait()
        low = jnp.dot(layer_v[s, :], in_v[...], preferred_element_type=F32).astype(BF16)
        in_t[:, s] = low.astype(F32).T
    width = in_t.shape[0]
    seqs = mask.shape[0]
    span = width // parts
    me = lax.axis_index("feat")
    for (k, begin, size), out in zip(ask, outs):
        small = math.gcd(ROW_BLOCK, size)
        base = pl.multiple_of((me ^ k) * span + begin, 8)
        for r in range(0, size, small):
            rows = in_t[pl.ds(base + r, small), :]
            left = (rows[:, None, :] * mask[...][None]).astype(BF16).reshape(small * seqs, tokens)
            got = jnp.dot(left, out_low[...], preferred_element_type=F32).astype(BF16)
            out[pl.ds(r, small)] = got.reshape(small, seqs, got.shape[1])


def grads(parts, ask, layer_in, grad_out, in_proj, out_proj, seq_ids, valid_counts):
    tokens, model = layer_in.shape
    width = in_proj.shape[1]
    seqs = valid_counts.shape[0]
    block = min(TOKEN_BLOCK, tokens)
    args = (layer_in, grad_out, in_proj, out_proj, seq_ids, valid_counts.reshape(1, seqs))
    return pl.pallas_call(
        functools.partial(grads_kernel, parts, ask),
        in_specs=[IN_HBM] * 6,
        out_specs=[IN_VMEM] * len(ask),
        out_shape=[pltpu.VMEM((size, seqs, width), BF16) for _, _, size in ask],
        scratch_shapes=[
            pltpu.VMEM((tokens, model), BF16),
            pltpu.VMEM((tokens, model), BF16),
            pltpu.VMEM((model, width), BF16),
            pltpu.VMEM((model, width), BF16),
            pltpu.VMEM((1, tokens), jnp.int32),
            pltpu.VMEM((1, seqs), jnp.int32),
            pltpu.VMEM((width, tokens), F32),
            pltpu.VMEM((tokens, width), BF16),
            pltpu.VMEM((seqs, tokens), F32),
            pltpu.SemaphoreType.DMA((4 + 2 * (tokens // block),)),
        ],
        compiler_params=PARAMS,
        cost_estimate=FREE,
        name="sequence_grads",
    )(*map(hbm, args))


def picked(total, order, parts):
    cols, q_rows = total.shape
    high = total.astype(BF16)
    left = total - high.astype(F32)
    middle = left.astype(BF16)
    low = (left - middle.astype(F32)).astype(BF16)
    wanted = lax.rem(order, q_rows)
    pick = (lax.broadcasted_iota(jnp.int32, (q_rows, q_rows), 0) == wanted).astype(F32).astype(BF16)
    got = jnp.dot(jnp.concatenate([high, middle, low], axis=0), pick, preferred_element_type=F32)
    got = got[:cols] + (got[cols:2 * cols] + got[2 * cols:])
    rows = q_rows // parts
    return [got[:, m * rows:(m + 1) * rows] for m in range(parts)]


def near_kernel(parts, count, own, other, own_order, other_order, *rest):
    pieces, sent = rest[:count], rest[count:count + parts]
    turned, held, sems = rest[count + parts:]
    size, _, width = pieces[0].shape
    slots, _, span = held.shape
    block = span // width
    steps = [(start, n) for start in range(0, size, block) for n in range(2)]

    def fetch(at):
        start, n = steps[at]
        source = (own, other)[n].at[:, pl.ds(start * width, span)]
        copy = pltpu.make_async_copy(source, held.at[at % slots], sems.at[at % slots])
        copy.start()
        return copy

    copies = [fetch(at) for at in range(min(slots, len(steps)))]
    totals = [None, None]
    for at, (start, n) in enumerate(steps):
        copies[at].wait()
        flipped = held[at % slots].T
        turned[n, pl.ds(start * width, span), :] = flipped
        for i in range(block):
            left = jnp.concatenate([piece[start + i] for piece in pieces], axis=0)
            got = jnp.dot(left, flipped[i * width:(i + 1) * width, :], preferred_element_type=F32)
            totals[n] = got if totals[n] is None else totals[n] + got
        if at + slots < len(steps):
            copies.append(fetch(at + slots))
    rows = sent[0].shape[1] // 2
    for n, order in enumerate((own_order, other_order)):
        for out, got in zip(sent, picked(totals[n], order[...], parts)):
            out[:, n * rows:(n + 1) * rows] = got


def near_scores(parts, queries, orders, pieces):
    size, seqs, width = pieces[0].shape
    q_rows = queries[0].shape[0]
    cols = len(pieces) * seqs
    block = min(QUERY_BLOCK, size)
    shapes = [jax.ShapeDtypeStruct((cols, 2 * q_rows // parts), F32)] * parts
    shapes += [pltpu.VMEM((2, size * width, q_rows), BF16)]
    done = pl.pallas_call(
        functools.partial(near_kernel, parts, len(pieces)),
        in_specs=[IN_HBM] * 2 + [IN_VMEM] * (2 + len(pieces)),
        out_specs=[IN_VMEM] * len(shapes),
        out_shape=shapes,
        scratch_shapes=[
            pltpu.VMEM((QUERY_SLOTS, q_rows, block * width), BF16),
            pltpu.SemaphoreType.DMA((QUERY_SLOTS,)),
        ],
        compiler_params=PARAMS,
        cost_estimate=FREE,
        name="near_scores",
    )(*map(hbm, queries), *orders, *pieces)
    return done[:parts], done[parts]


def part_kernel(turned, *rest):
    pieces, out = rest[:-1], rest[-1]
    size, _, width = pieces[-1].shape
    for n in range(2):
        total = None
        for i in range(size):
            left = jnp.concatenate([piece[i] for piece in pieces], axis=0)
            got = jnp.dot(left, turned[n, i * width:(i + 1) * width, :], preferred_element_type=F32)
            total = got if total is None else total + got
        out[n] = total


def part_scores(turned, pieces):
    args = [turned, *pieces]
    return pl.pallas_call(
        part_kernel,
        in_specs=[IN_VMEM] * len(args),
        out_specs=IN_VMEM,
        out_shape=jax.ShapeDtypeStruct((2, len(pieces) * pieces[0].shape[1], turned.shape[2]), F32),
        compiler_params=SMALL,
        cost_estimate=FREE,
        name="part_scores",
    )(*args)


def late_kernel(count, first, turned, before, own_order, other_order, *rest):
    pieces, sent = rest[:count], rest[count:]
    size, _, width = pieces[-1].shape
    totals = [before[0], before[1]]
    for i in range(size):
        left = jnp.concatenate([piece[i + first if piece.shape[0] > size else i] for piece in pieces], axis=0)
        for n in range(2):
            right = turned[n, (first + i) * width:(first + i + 1) * width, :]
            totals[n] = totals[n] + jnp.dot(left, right, preferred_element_type=F32)
    rows = sent[0].shape[1] // 2
    for n, order in enumerate((own_order, other_order)):
        for out, got in zip(sent, picked(totals[n], order[...], len(sent))):
            out[:, n * rows:(n + 1) * rows] = got


def late_scores(parts, first, turned, before, orders, pieces):
    cols, q_rows = before.shape[1:]
    args = [turned, before, *orders, *pieces]
    shapes = [jax.ShapeDtypeStruct((cols, 2 * q_rows // parts), F32)] * parts
    return pl.pallas_call(
        functools.partial(late_kernel, len(pieces), first),
        in_specs=[IN_VMEM] * len(args),
        out_specs=[IN_VMEM] * parts,
        out_shape=shapes,
        compiler_params=SMALL,
        cost_estimate=FREE,
        name="late_scores",
    )(*args)


def reduce_kernel(parts, crossing, seqs, sets, *refs):
    own, other = refs[-2:]
    rows = own.shape[1]
    where = {k: (g, n) for g, ks in enumerate(sets) for n, k in enumerate(ks)}
    size = crossing * seqs
    for k in range(parts):
        total = None
        for m in range(parts):
            g, n = where[k ^ m]
            got = refs[g * parts + m][pl.ds(n * size, size), :]
            total = got if total is None else total + got
        own[pl.ds(k * size, size), :] = total[:, :rows]
        other[pl.ds(k * size, size), :] = total[:, rows:]


def reduce(parts, crossing, seqs, sets, messages):
    flat = [message for group in messages for message in group]
    shape = jax.ShapeDtypeStruct((parts * crossing * seqs, flat[0].shape[1] // 2), F32)
    return pl.pallas_call(
        functools.partial(reduce_kernel, parts, crossing, seqs, sets),
        in_specs=[IN_VMEM] * len(flat),
        out_specs=[IN_VMEM] * 2,
        out_shape=[shape] * 2,
        compiler_params=PARAMS,
        cost_estimate=FREE,
        name="reduce",
    )(*flat)


def finish_kernel(parts, dp, seqs, own, other, out, columns):
    z, d = lax.axis_index("feat"), lax.axis_index("dp")
    crossed = (0, dp // 2)
    for k in range(parts):
        for n, e in enumerate(crossed):
            for flip, ref in ((0, own), (1, other)):
                place = ((d ^ e ^ flip) * parts + (z ^ k)) * seqs
                rows = ref[pl.ds((k * len(crossed) + n) * seqs, seqs), :]
                columns[pl.ds(pl.multiple_of(place, seqs), seqs), :] = rows
    out[...] = columns[...].T


def finish(parts, dp, seqs, own, other):
    rows = own.shape[1]
    total = parts * dp * seqs
    return pl.pallas_call(
        functools.partial(finish_kernel, parts, dp, seqs),
        in_specs=[IN_VMEM] * 2,
        out_specs=IN_VMEM,
        out_shape=jax.ShapeDtypeStruct((rows, total), F32),
        scratch_shapes=[pltpu.VMEM((total, rows), F32)],
        compiler_params=PARAMS,
        cost_estimate=FREE,
        name="finish",
    )(own, other)


def swap(array, axis, size, by):
    return lax.ppermute(array, axis, [(i, i ^ by) for i in range(size)])


def after(array, *earlier):
    return lax.optimization_barrier((array, *earlier))[0]


def direct(parts, dp, layer_in, grad_out, in_proj, out_proj, queries, seq_ids, valid_counts, owner_order):
    seqs = valid_counts.shape[0]
    span = in_proj.shape[1] // parts
    cut = span * SPLIT // 8
    me = lax.axis_index("feat")
    cross = lambda array: swap(array, "dp", dp, dp // 2)
    pair = lambda array: swap(array, "dp", dp, 1)
    move = lambda array, k: swap(array, "feat", parts, k)
    order = jnp.take(owner_order.reshape(parts, -1), me ^ jnp.arange(parts), axis=0).reshape(1, -1)
    orders = [order, pair(order)]
    ask = [(1, 0, span), (2, 0, span), (3, 0, cut), (0, 0, span), (3, cut, span - cut)]
    g1, g2, g3a, g0, g3b = grads(parts, ask, layer_in, grad_out, in_proj, out_proj, seq_ids, valid_counts)
    both = [queries, pair(queries)]
    x0 = cross(g0)
    z1 = move(g1, 1)
    z2 = move(g2, 2)
    z3a = move(g3a, 3)
    x1 = cross(z1)
    near, turned = near_scores(parts, both, orders, [g0, x0, z1, x1])
    z3b = move(after(g3b, x0), 3)
    x2 = cross(after(z2, x0))
    x3a = cross(z3a)
    x3b = cross(after(z3b, near[0]))
    sent = [near[0]] + [move(near[m], m) for m in range(1, parts)]
    part = part_scores(turned, [z2, x2, z3a, x3a])
    far = late_scores(parts, cut, turned, part, orders, [z2, x2, z3b, x3b])
    messages = [sent, [far[0]] + [move(far[m], m) for m in range(1, parts)]]
    own, other = reduce(parts, 2, seqs, [[0, 1], [2, 3]], messages)
    return finish(parts, dp, seqs, own, pair(other))


def gathered(parts, dp, layer_in, grad_out, in_proj, out_proj, queries, seq_ids, valid_counts, owner_order):
    span = in_proj.shape[1] // parts
    ask = [(k, 0, span) for k in range(parts)]
    own = jnp.stack(grads(parts, ask, layer_in, grad_out, in_proj, out_proj, seq_ids, valid_counts))
    own = jnp.take(own, lax.axis_index("feat") ^ jnp.arange(parts), axis=0)
    size = own.shape[1]
    rows = lax.all_to_all(own, "feat", split_axis=0, concat_axis=0, tiled=True)
    rows = lax.all_gather(rows, "dp", axis=0, tiled=True)
    q_rows = queries.shape[0]
    by_row = queries.reshape(q_rows, size, -1)
    scored = jnp.einsum("qij,gisj->qgs", by_row, rows, preferred_element_type=F32)
    scored = jnp.take(scored.reshape(q_rows, -1), owner_order % q_rows, axis=0)
    return lax.psum_scatter(scored, "feat", scatter_dimension=0, tiled=True)


def solution(mesh):
    parts, dp = mesh.shape["feat"], mesh.shape["dp"]
    in_specs = (
        P(("dom", "dp", "feat"), None),
        P(("dom", "dp", "feat"), None),
        P(),
        P(),
        P(("dom", "dp"), "feat"),
        P(("dom", "dp", "feat"), None),
        P(("dom", "dp", "feat")),
        P(("dom", "dp")),
    )
    out_specs = P(("dom", "dp", "feat"), None)
    body = functools.partial(direct if parts == 4 and dp == 4 else gathered, parts, dp)
    return jax.shard_map(body, mesh=mesh, in_specs=in_specs, out_specs=out_specs, check_vma=False)
```

```python
import functools
import math

import jax
import jax.numpy as jnp
from jax import lax
from jax.experimental import pallas as pl
from jax.experimental.pallas import tpu as pltpu
from jax.sharding import PartitionSpec as P

F32 = jnp.float32
BF16 = jnp.bfloat16
NT = (((1,), (1,)), ((), ()))
MIB = 1 << 20
TOKEN_BLOCK = 512
ROW_BLOCK = 16
QUERY_BLOCK = 8
SPLIT = 4
QUERY_SLOTS = 8
FREE = pl.CostEstimate(flops=0, bytes_accessed=0, transcendentals=0)
IN_HBM = pl.BlockSpec(memory_space=pltpu.HBM)
IN_VMEM = pl.BlockSpec(memory_space=pltpu.VMEM)
SMALL = pltpu.CompilerParams(vmem_limit_bytes=6 * MIB)
PARAMS = pltpu.CompilerParams(vmem_limit_bytes=16 * MIB)


def hbm(array):
    return pltpu.with_memory_space_constraint(array, pltpu.HBM)


def counted_mask(ids, valid):
    seqs, tokens = valid.shape[1], ids.shape[1]
    eye = lax.broadcasted_iota(jnp.int32, (seqs, seqs), 0) == lax.broadcasted_iota(jnp.int32, (seqs, seqs), 1)
    limit = jnp.sum(jnp.where(eye, jnp.broadcast_to(valid, (seqs, seqs)), 0), axis=1, keepdims=True)
    ids = jnp.broadcast_to(ids, (seqs, tokens))
    seq = lax.broadcasted_iota(jnp.int32, (seqs, tokens), 0)
    start = jnp.sum((ids < seq).astype(jnp.int32), axis=1, keepdims=True)
    position = lax.broadcasted_iota(jnp.int32, (seqs, tokens), 1) - start
    return jnp.where((ids == seq) & (position < limit), 1.0, 0.0).astype(F32)


def slice_grads(parts, ask, in_t, out_low, mask, outs):
    width, tokens = in_t.shape
    seqs = mask.shape[0]
    span = width // parts
    me = lax.axis_index("feat")
    for (k, begin, size), out in zip(ask, outs):
        small = math.gcd(ROW_BLOCK, size)
        base = pl.multiple_of((me ^ k) * span + begin, 8)
        for r in range(0, size, small):
            rows = in_t[pl.ds(base + r, small), :]
            left = (rows[:, None, :] * mask[...][None]).astype(BF16).reshape(small * seqs, tokens)
            got = jnp.dot(left, out_low[...], preferred_element_type=F32).astype(BF16)
            out[pl.ds(r, small)] = got.reshape(small, seqs, got.shape[1])


def project_kernel(parts, ask, layer, grad, in_proj, out_proj, ids, valid, in_t, out_low, mask, *rest):
    outs = rest[: len(ask)]
    layer_v, grad_v, in_v, out_v, ids_v, valid_v, sems = rest[len(ask):]
    tokens = layer.shape[0]
    block = min(TOKEN_BLOCK, tokens)
    spans = [pl.ds(t, block) for t in range(0, tokens, block)]
    copies = []

    def fetch(source, target, at):
        copy = pltpu.make_async_copy(source, target, sems.at[at])
        copy.start()
        copies.append(copy)
        return copy

    out_copy = fetch(out_proj, out_v, 0)
    grad_copies = [fetch(grad.at[spans[0]], grad_v.at[spans[0]], 4)]
    small_copies = [fetch(ids, ids_v, 1), fetch(valid, valid_v, 2)]
    grad_copies += [fetch(grad.at[s], grad_v.at[s], 5 + n) for n, s in enumerate(spans[1:])]
    in_copy = fetch(in_proj, in_v, 3)
    layer_copies = [fetch(layer.at[s], layer_v.at[s], 4 + len(spans) + n) for n, s in enumerate(spans)]
    for copy in small_copies:
        copy.wait()
    mask[...] = counted_mask(ids_v[...], valid_v[...])
    out_copy.wait()
    @pl.loop(0, len(spans))
    def _(n):
        s = pl.ds(pl.multiple_of(n * block, block), block)
        pltpu.make_async_copy(grad.at[s], grad_v.at[s], sems.at[4 + n]).wait()
        out_low[s, :] = jnp.dot(grad_v[s, :], out_v[...], preferred_element_type=F32).astype(BF16)
    in_copy.wait()
    @pl.loop(0, len(spans))
    def _(n):
        s = pl.ds(pl.multiple_of(n * block, block), block)
        pltpu.make_async_copy(layer.at[s], layer_v.at[s], sems.at[4 + len(spans) + n]).wait()
        low = jnp.dot(layer_v[s, :], in_v[...], preferred_element_type=F32).astype(BF16)
        in_t[:, s] = low.astype(F32).T
    slice_grads(parts, ask, in_t, out_low, mask, outs)


def piece_shapes(ask, seqs, width):
    return [(pltpu.HBM if late else pltpu.VMEM)((size, seqs, width), BF16) for _, _, size, late in ask]


def project(parts, ask, layer_in, grad_out, in_proj, out_proj, seq_ids, valid_counts):
    tokens, model = layer_in.shape
    width = in_proj.shape[1]
    seqs = valid_counts.shape[0]
    block = min(TOKEN_BLOCK, tokens)
    args = (layer_in, grad_out, in_proj, out_proj, seq_ids, valid_counts.reshape(1, seqs))
    shapes = [pltpu.VMEM((width, tokens), F32), pltpu.VMEM((tokens, width), BF16), pltpu.VMEM((seqs, tokens), F32)]
    shapes += piece_shapes(ask, seqs, width)
    done = pl.pallas_call(
        functools.partial(project_kernel, parts, [part[:3] for part in ask]),
        in_specs=[IN_HBM] * 6,
        out_specs=[IN_VMEM] * len(shapes),
        out_shape=shapes,
        scratch_shapes=[
            pltpu.VMEM((tokens, model), BF16),
            pltpu.VMEM((tokens, model), BF16),
            pltpu.VMEM((model, width), BF16),
            pltpu.VMEM((model, width), BF16),
            pltpu.VMEM((1, tokens), jnp.int32),
            pltpu.VMEM((1, seqs), jnp.int32),
            pltpu.SemaphoreType.DMA((4 + 2 * (tokens // block),)),
        ],
        compiler_params=PARAMS,
        cost_estimate=FREE,
        name="project",
    )(*map(hbm, args))
    return done[:3], done[3:]


def grads_kernel(parts, ask, in_t, out_low, mask, *outs):
    slice_grads(parts, ask, in_t, out_low, mask, outs)


def grads(parts, ask, in_t, out_low, mask):
    tokens, width = out_low.shape
    return pl.pallas_call(
        functools.partial(grads_kernel, parts, [part[:3] for part in ask]),
        in_specs=[IN_VMEM] * 3,
        out_specs=[IN_VMEM] * len(ask),
        out_shape=piece_shapes(ask, mask.shape[0], width),
        compiler_params=SMALL,
        cost_estimate=FREE,
        name="sequence_grads",
    )(in_t, out_low, mask)


def picked(total, order, parts):
    cols, q_rows = total.shape
    high = total.astype(BF16)
    left = total - high.astype(F32)
    middle = left.astype(BF16)
    low = (left - middle.astype(F32)).astype(BF16)
    wanted = lax.rem(order, q_rows)
    pick = (lax.broadcasted_iota(jnp.int32, (q_rows, q_rows), 0) == wanted).astype(F32).astype(BF16)
    got = jnp.dot(jnp.concatenate([high, middle, low], axis=0), pick, preferred_element_type=F32)
    got = got[:cols] + (got[cols:2 * cols] + got[2 * cols:])
    rows = q_rows // parts
    return [got[:, m * rows:(m + 1) * rows] for m in range(parts)]


def near_kernel(parts, count, own, other, own_order, other_order, *rest):
    pieces, sent = rest[:count], rest[count:count + parts]
    turned, held, sems = rest[count + parts:]
    size, _, width = pieces[0].shape
    slots, _, span = held.shape
    block = span // width
    steps = [(start, n) for start in range(0, size, block) for n in range(2)]

    def fetch(at):
        start, n = steps[at]
        source = (own, other)[n].at[:, pl.ds(start * width, span)]
        copy = pltpu.make_async_copy(source, held.at[at % slots], sems.at[at % slots])
        copy.start()
        return copy

    copies = [fetch(at) for at in range(min(slots, len(steps)))]
    totals = [None, None]
    for at, (start, n) in enumerate(steps):
        copies[at].wait()
        flipped = held[at % slots].T
        turned[n, pl.ds(start * width, span), :] = flipped
        for i in range(block):
            left = jnp.concatenate([piece[start + i] for piece in pieces], axis=0)
            got = jnp.dot(left, flipped[i * width:(i + 1) * width, :], preferred_element_type=F32)
            totals[n] = got if totals[n] is None else totals[n] + got
        if at + slots < len(steps):
            copies.append(fetch(at + slots))
    rows = sent[0].shape[1] // 2
    for n, order in enumerate((own_order, other_order)):
        for out, got in zip(sent, picked(totals[n], order[...], parts)):
            out[:, n * rows:(n + 1) * rows] = got


def near_scores(parts, queries, orders, pieces):
    size, seqs, width = pieces[0].shape
    q_rows = queries[0].shape[0]
    cols = len(pieces) * seqs
    block = min(QUERY_BLOCK, size)
    shapes = [jax.ShapeDtypeStruct((cols, 2 * q_rows // parts), F32)] * parts
    shapes += [pltpu.VMEM((2, size * width, q_rows), BF16)]
    done = pl.pallas_call(
        functools.partial(near_kernel, parts, len(pieces)),
        in_specs=[IN_HBM] * 2 + [IN_VMEM] * (2 + len(pieces)),
        out_specs=[IN_VMEM] * len(shapes),
        out_shape=shapes,
        scratch_shapes=[
            pltpu.VMEM((QUERY_SLOTS, q_rows, block * width), BF16),
            pltpu.SemaphoreType.DMA((QUERY_SLOTS,)),
        ],
        compiler_params=PARAMS,
        cost_estimate=FREE,
        name="near_scores",
    )(*map(hbm, queries), *orders, *pieces)
    return done[:parts], done[parts]


def part_kernel(turned, *rest):
    pieces, out = rest[:-1], rest[-1]
    size, _, width = pieces[-1].shape
    for n in range(2):
        total = None
        for i in range(size):
            left = jnp.concatenate([piece[i] for piece in pieces], axis=0)
            got = jnp.dot(left, turned[n, i * width:(i + 1) * width, :], preferred_element_type=F32)
            total = got if total is None else total + got
        out[n] = total


def part_scores(turned, pieces):
    args = [turned, *pieces]
    return pl.pallas_call(
        part_kernel,
        in_specs=[IN_VMEM] * len(args),
        out_specs=IN_VMEM,
        out_shape=jax.ShapeDtypeStruct((2, len(pieces) * pieces[0].shape[1], turned.shape[2]), F32),
        compiler_params=SMALL,
        cost_estimate=FREE,
        name="part_scores",
    )(*args)


def late_kernel(count, first, turned, before, own_order, other_order, *rest):
    pieces, sent = rest[:count], rest[count:]
    size, _, width = pieces[-1].shape
    totals = [before[0], before[1]]
    for i in range(size):
        left = jnp.concatenate([piece[i + first if piece.shape[0] > size else i] for piece in pieces], axis=0)
        for n in range(2):
            right = turned[n, (first + i) * width:(first + i + 1) * width, :]
            totals[n] = totals[n] + jnp.dot(left, right, preferred_element_type=F32)
    rows = sent[0].shape[1] // 2
    for n, order in enumerate((own_order, other_order)):
        for out, got in zip(sent, picked(totals[n], order[...], len(sent))):
            out[:, n * rows:(n + 1) * rows] = got


def late_scores(parts, first, turned, before, orders, pieces):
    cols, q_rows = before.shape[1:]
    args = [turned, before, *orders, *pieces]
    shapes = [jax.ShapeDtypeStruct((cols, 2 * q_rows // parts), F32)] * parts
    return pl.pallas_call(
        functools.partial(late_kernel, len(pieces), first),
        in_specs=[IN_VMEM] * len(args),
        out_specs=[IN_VMEM] * parts,
        out_shape=shapes,
        compiler_params=SMALL,
        cost_estimate=FREE,
        name="late_scores",
    )(*args)


def reduce_kernel(parts, crossing, seqs, sets, *refs):
    own, other = refs[-2:]
    rows = own.shape[1]
    where = {key: (g, n) for g, keys in enumerate(sets) for n, key in enumerate(keys)}
    for k in range(parts):
        for e in range(crossing):
            total = None
            for m in range(parts):
                g, n = where[k ^ m, e]
                got = refs[g * parts + m][pl.ds(n * seqs, seqs), :]
                total = got if total is None else total + got
            place = pl.ds((k * crossing + e) * seqs, seqs)
            own[place, :] = total[:, :rows]
            other[place, :] = total[:, rows:]


def reduce(parts, crossing, seqs, sets, messages):
    flat = [message for group in messages for message in group]
    shape = jax.ShapeDtypeStruct((parts * crossing * seqs, flat[0].shape[1] // 2), F32)
    return pl.pallas_call(
        functools.partial(reduce_kernel, parts, crossing, seqs, sets),
        in_specs=[IN_VMEM] * len(flat),
        out_specs=[IN_VMEM] * 2,
        out_shape=[shape] * 2,
        compiler_params=PARAMS,
        cost_estimate=FREE,
        name="reduce",
    )(*flat)


def finish_kernel(parts, dp, seqs, own, other, out, columns):
    z, d = lax.axis_index("feat"), lax.axis_index("dp")
    crossed = (0, dp // 2)
    for k in range(parts):
        for n, e in enumerate(crossed):
            for flip, ref in ((0, own), (1, other)):
                place = ((d ^ e ^ flip) * parts + (z ^ k)) * seqs
                rows = ref[pl.ds((k * len(crossed) + n) * seqs, seqs), :]
                columns[pl.ds(pl.multiple_of(place, seqs), seqs), :] = rows
    out[...] = columns[...].T


def finish(parts, dp, seqs, own, other):
    rows = own.shape[1]
    total = parts * dp * seqs
    return pl.pallas_call(
        functools.partial(finish_kernel, parts, dp, seqs),
        in_specs=[IN_VMEM] * 2,
        out_specs=IN_VMEM,
        out_shape=jax.ShapeDtypeStruct((rows, total), F32),
        scratch_shapes=[pltpu.VMEM((total, rows), F32)],
        compiler_params=PARAMS,
        cost_estimate=FREE,
        name="finish",
    )(own, other)


def swap(array, axis, size, by):
    return lax.ppermute(array, axis, [(i, i ^ by) for i in range(size)])


def after(array, *earlier):
    return lax.optimization_barrier((array, *earlier))[0]


def direct(parts, dp, layer_in, grad_out, in_proj, out_proj, queries, seq_ids, valid_counts, owner_order):
    seqs = valid_counts.shape[0]
    span = in_proj.shape[1] // parts
    cut = span * SPLIT // 8
    me = lax.axis_index("feat")
    cross = lambda array: swap(array, "dp", dp, dp // 2)
    pair = lambda array: swap(array, "dp", dp, 1)
    move = lambda array, k: swap(array, "feat", parts, k)
    order = jnp.take(owner_order.reshape(parts, -1), me ^ jnp.arange(parts), axis=0).reshape(1, -1)
    orders = [order, pair(order)]
    low, (g2, g1) = project(
        parts, [(2, 0, span, False), (1, 0, span, False)], layer_in, grad_out, in_proj, out_proj, seq_ids, valid_counts
    )
    g0, g3a, g3b = grads(parts, [(0, 0, span, False), (3, 0, cut, False), (3, cut, span - cut, True)], *low)
    both = [queries, pair(queries)]
    x0 = cross(g0)
    z1 = move(g1, 1)
    z2 = move(g2, 2)
    z3a = move(after(g3a, z1), 3)
    x1p = cross(g1)
    x1 = move(after(x1p, z1), 1)
    near, turned = near_scores(parts, both, orders, [g0, x0, z1, z2])
    z3b = move(after(g3b, z2), 3)
    x2 = cross(z2)
    x3a = cross(after(z3a, near[0]))
    x3b = cross(z3b)
    sent = [near[0]] + [move(near[m], m) for m in range(1, parts)]
    part = part_scores(turned, [x1, x2, z3a, x3a])
    far = late_scores(parts, cut, turned, part, orders, [x1, x2, z3b, x3b])
    messages = [sent, [far[0]] + [move(far[m], m) for m in range(1, parts)]]
    sets = [[(0, 0), (0, 1), (1, 0), (2, 0)], [(1, 1), (2, 1), (3, 0), (3, 1)]]
    own, other = reduce(parts, 2, seqs, sets, messages)
    return finish(parts, dp, seqs, own, pair(other))


def gathered(parts, dp, layer_in, grad_out, in_proj, out_proj, queries, seq_ids, valid_counts, owner_order):
    span = in_proj.shape[1] // parts
    ask = [(k, 0, span, False) for k in range(parts)]
    _, own = project(parts, ask, layer_in, grad_out, in_proj, out_proj, seq_ids, valid_counts)
    own = jnp.stack(own)
    own = jnp.take(own, lax.axis_index("feat") ^ jnp.arange(parts), axis=0)
    size = own.shape[1]
    rows = lax.all_to_all(own, "feat", split_axis=0, concat_axis=0, tiled=True)
    rows = lax.all_gather(rows, "dp", axis=0, tiled=True)
    q_rows = queries.shape[0]
    by_row = queries.reshape(q_rows, size, -1)
    scored = jnp.einsum("qij,gisj->qgs", by_row, rows, preferred_element_type=F32)
    scored = jnp.take(scored.reshape(q_rows, -1), owner_order % q_rows, axis=0)
    return lax.psum_scatter(scored, "feat", scatter_dimension=0, tiled=True)


def solution(mesh):
    parts, dp = mesh.shape["feat"], mesh.shape["dp"]
    in_specs = (
        P(("dom", "dp", "feat"), None),
        P(("dom", "dp", "feat"), None),
        P(),
        P(),
        P(("dom", "dp"), "feat"),
        P(("dom", "dp", "feat"), None),
        P(("dom", "dp", "feat")),
        P(("dom", "dp")),
    )
    out_specs = P(("dom", "dp", "feat"), None)
    body = functools.partial(direct if parts == 4 and dp == 4 else gathered, parts, dp)
    return jax.shard_map(body, mesh=mesh, in_specs=in_specs, out_specs=out_specs, check_vma=False)
```

```python
import functools
import math

import jax
import jax.numpy as jnp
from jax import lax
from jax.experimental import pallas as pl
from jax.experimental.pallas import tpu as pltpu
from jax.sharding import PartitionSpec as P

F32 = jnp.float32
BF16 = jnp.bfloat16
NT = (((1,), (1,)), ((), ()))
MIB = 1 << 20
TOKEN_BLOCK = 512
ROW_BLOCK = 16
QUERY_BLOCK = 8
SPLIT = 4
QUERY_SLOTS = 8
FREE = pl.CostEstimate(flops=0, bytes_accessed=0, transcendentals=0)
IN_HBM = pl.BlockSpec(memory_space=pltpu.HBM)
IN_VMEM = pl.BlockSpec(memory_space=pltpu.VMEM)
SMALL = pltpu.CompilerParams(vmem_limit_bytes=6 * MIB)
PARAMS = pltpu.CompilerParams(vmem_limit_bytes=16 * MIB)


def hbm(array):
    return pltpu.with_memory_space_constraint(array, pltpu.HBM)


def counted_mask(ids, valid):
    seqs, tokens = valid.shape[1], ids.shape[1]
    eye = lax.broadcasted_iota(jnp.int32, (seqs, seqs), 0) == lax.broadcasted_iota(jnp.int32, (seqs, seqs), 1)
    limit = jnp.sum(jnp.where(eye, jnp.broadcast_to(valid, (seqs, seqs)), 0), axis=1, keepdims=True)
    ids = jnp.broadcast_to(ids, (seqs, tokens))
    seq = lax.broadcasted_iota(jnp.int32, (seqs, tokens), 0)
    start = jnp.sum((ids < seq).astype(jnp.int32), axis=1, keepdims=True)
    position = lax.broadcasted_iota(jnp.int32, (seqs, tokens), 1) - start
    return jnp.where((ids == seq) & (position < limit), 1.0, 0.0).astype(F32)


def slice_grads(parts, ask, in_t, out_low, mask, outs):
    width, tokens = in_t.shape
    seqs = mask.shape[0]
    span = width // parts
    me = lax.axis_index("feat")
    for (k, begin, size), out in zip(ask, outs):
        small = math.gcd(ROW_BLOCK, size)
        base = pl.multiple_of((me ^ k) * span + begin, 8)
        for r in range(0, size, small):
            rows = in_t[pl.ds(base + r, small), :]
            left = (rows[:, None, :] * mask[...][None]).astype(BF16).reshape(small * seqs, tokens)
            got = jnp.dot(left, out_low[...], preferred_element_type=F32).astype(BF16)
            out[pl.ds(r, small)] = got.reshape(small, seqs, got.shape[1])


def project_kernel(parts, ask, layer, grad, in_proj, out_proj, ids, valid, in_t, out_low, mask, *rest):
    outs = rest[: len(ask)]
    layer_v, grad_v, in_v, out_v, ids_v, valid_v, sems = rest[len(ask):]
    tokens = layer.shape[0]
    block = min(TOKEN_BLOCK, tokens)
    spans = [pl.ds(t, block) for t in range(0, tokens, block)]
    copies = []

    def fetch(source, target, at):
        copy = pltpu.make_async_copy(source, target, sems.at[at])
        copy.start()
        copies.append(copy)
        return copy

    out_copy = fetch(out_proj, out_v, 0)
    grad_copies = [fetch(grad.at[spans[0]], grad_v.at[spans[0]], 4)]
    small_copies = [fetch(ids, ids_v, 1), fetch(valid, valid_v, 2)]
    grad_copies += [fetch(grad.at[s], grad_v.at[s], 5 + n) for n, s in enumerate(spans[1:])]
    in_copy = fetch(in_proj, in_v, 3)
    layer_copies = [fetch(layer.at[s], layer_v.at[s], 4 + len(spans) + n) for n, s in enumerate(spans)]
    for copy in small_copies:
        copy.wait()
    mask[...] = counted_mask(ids_v[...], valid_v[...])
    out_copy.wait()
    @pl.loop(0, len(spans))
    def _(n):
        s = pl.ds(pl.multiple_of(n * block, block), block)
        pltpu.make_async_copy(grad.at[s], grad_v.at[s], sems.at[4 + n]).wait()
        out_low[s, :] = jnp.dot(grad_v[s, :], out_v[...], preferred_element_type=F32).astype(BF16)
    in_copy.wait()
    @pl.loop(0, len(spans))
    def _(n):
        s = pl.ds(pl.multiple_of(n * block, block), block)
        pltpu.make_async_copy(layer.at[s], layer_v.at[s], sems.at[4 + len(spans) + n]).wait()
        low = jnp.dot(layer_v[s, :], in_v[...], preferred_element_type=F32).astype(BF16)
        in_t[:, s] = low.astype(F32).T
    slice_grads(parts, ask, in_t, out_low, mask, outs)


def piece_shapes(ask, seqs, width):
    return [(pltpu.HBM if late else pltpu.VMEM)((size, seqs, width), BF16) for _, _, size, late in ask]


def project(parts, ask, layer_in, grad_out, in_proj, out_proj, seq_ids, valid_counts):
    tokens, model = layer_in.shape
    width = in_proj.shape[1]
    seqs = valid_counts.shape[0]
    block = min(TOKEN_BLOCK, tokens)
    args = (layer_in, grad_out, in_proj, out_proj, seq_ids, valid_counts.reshape(1, seqs))
    shapes = [pltpu.VMEM((width, tokens), F32), pltpu.VMEM((tokens, width), BF16), pltpu.VMEM((seqs, tokens), F32)]
    shapes += piece_shapes(ask, seqs, width)
    done = pl.pallas_call(
        functools.partial(project_kernel, parts, [part[:3] for part in ask]),
        in_specs=[IN_HBM] * 6,
        out_specs=[IN_VMEM] * len(shapes),
        out_shape=shapes,
        scratch_shapes=[
            pltpu.VMEM((tokens, model), BF16),
            pltpu.VMEM((tokens, model), BF16),
            pltpu.VMEM((model, width), BF16),
            pltpu.VMEM((model, width), BF16),
            pltpu.VMEM((1, tokens), jnp.int32),
            pltpu.VMEM((1, seqs), jnp.int32),
            pltpu.SemaphoreType.DMA((4 + 2 * (tokens // block),)),
        ],
        compiler_params=PARAMS,
        cost_estimate=FREE,
        name="project",
    )(*map(hbm, args))
    return done[:3], done[3:]


def grads_kernel(parts, ask, in_t, out_low, mask, *outs):
    slice_grads(parts, ask, in_t, out_low, mask, outs)


def grads(parts, ask, in_t, out_low, mask):
    tokens, width = out_low.shape
    return pl.pallas_call(
        functools.partial(grads_kernel, parts, [part[:3] for part in ask]),
        in_specs=[IN_VMEM] * 3,
        out_specs=[IN_VMEM] * len(ask),
        out_shape=piece_shapes(ask, mask.shape[0], width),
        compiler_params=SMALL,
        cost_estimate=FREE,
        name="sequence_grads",
    )(in_t, out_low, mask)


def picked(total, order, parts):
    cols, q_rows = total.shape
    high = total.astype(BF16)
    left = total - high.astype(F32)
    middle = left.astype(BF16)
    low = (left - middle.astype(F32)).astype(BF16)
    wanted = lax.rem(order, q_rows)
    pick = (lax.broadcasted_iota(jnp.int32, (q_rows, q_rows), 0) == wanted).astype(F32).astype(BF16)
    got = jnp.dot(jnp.concatenate([high, middle, low], axis=0), pick, preferred_element_type=F32)
    got = got[:cols] + (got[cols:2 * cols] + got[2 * cols:])
    rows = q_rows // parts
    return [got[:, m * rows:(m + 1) * rows] for m in range(parts)]


def near_kernel(parts, count, own, other, own_order, other_order, *rest):
    pieces, sent = rest[:count], rest[count:count + parts]
    turned, held, sems = rest[count + parts:]
    size, _, width = pieces[0].shape
    slots, _, span = held.shape
    block = span // width
    steps = [(start, n) for start in range(0, size, block) for n in range(2)]

    def fetch(at):
        start, n = steps[at]
        source = (own, other)[n].at[:, pl.ds(start * width, span)]
        copy = pltpu.make_async_copy(source, held.at[at % slots], sems.at[at % slots])
        copy.start()
        return copy

    copies = [fetch(at) for at in range(min(slots, len(steps)))]
    totals = [None, None]
    for at, (start, n) in enumerate(steps):
        copies[at].wait()
        flipped = held[at % slots].T
        turned[n, pl.ds(start * width, span), :] = flipped
        for i in range(block):
            left = jnp.concatenate([piece[start + i] for piece in pieces], axis=0)
            got = jnp.dot(left, flipped[i * width:(i + 1) * width, :], preferred_element_type=F32)
            totals[n] = got if totals[n] is None else totals[n] + got
        if at + slots < len(steps):
            copies.append(fetch(at + slots))
    rows = sent[0].shape[1] // 2
    for n, order in enumerate((own_order, other_order)):
        for out, got in zip(sent, picked(totals[n], order[...], parts)):
            out[:, n * rows:(n + 1) * rows] = got


def near_scores(parts, queries, orders, pieces):
    size, seqs, width = pieces[0].shape
    q_rows = queries[0].shape[0]
    cols = len(pieces) * seqs
    block = min(QUERY_BLOCK, size)
    shapes = [jax.ShapeDtypeStruct((cols, 2 * q_rows // parts), F32)] * parts
    shapes += [pltpu.VMEM((2, size * width, q_rows), BF16)]
    done = pl.pallas_call(
        functools.partial(near_kernel, parts, len(pieces)),
        in_specs=[IN_HBM] * 2 + [IN_VMEM] * (2 + len(pieces)),
        out_specs=[IN_VMEM] * len(shapes),
        out_shape=shapes,
        scratch_shapes=[
            pltpu.VMEM((QUERY_SLOTS, q_rows, block * width), BF16),
            pltpu.SemaphoreType.DMA((QUERY_SLOTS,)),
        ],
        compiler_params=PARAMS,
        cost_estimate=FREE,
        name="near_scores",
    )(*map(hbm, queries), *orders, *pieces)
    return done[:parts], done[parts]


def part_kernel(turned, *rest):
    pieces, out = rest[:-1], rest[-1]
    size, _, width = pieces[-1].shape
    for n in range(2):
        total = None
        for i in range(size):
            left = jnp.concatenate([piece[i] for piece in pieces], axis=0)
            got = jnp.dot(left, turned[n, i * width:(i + 1) * width, :], preferred_element_type=F32)
            total = got if total is None else total + got
        out[n] = total


def part_scores(turned, pieces):
    args = [turned, *pieces]
    return pl.pallas_call(
        part_kernel,
        in_specs=[IN_VMEM] * len(args),
        out_specs=IN_VMEM,
        out_shape=jax.ShapeDtypeStruct((2, len(pieces) * pieces[0].shape[1], turned.shape[2]), F32),
        compiler_params=SMALL,
        cost_estimate=FREE,
        name="part_scores",
    )(*args)


def late_kernel(count, first, turned, before, own_order, other_order, *rest):
    pieces, sent = rest[:count], rest[count:]
    size, _, width = pieces[-1].shape
    totals = [before[0], before[1]]
    for i in range(size):
        left = jnp.concatenate([piece[i + first if piece.shape[0] > size else i] for piece in pieces], axis=0)
        for n in range(2):
            right = turned[n, (first + i) * width:(first + i + 1) * width, :]
            totals[n] = totals[n] + jnp.dot(left, right, preferred_element_type=F32)
    rows = sent[0].shape[1] // 2
    for n, order in enumerate((own_order, other_order)):
        for out, got in zip(sent, picked(totals[n], order[...], len(sent))):
            out[:, n * rows:(n + 1) * rows] = got


def late_scores(parts, first, turned, before, orders, pieces):
    cols, q_rows = before.shape[1:]
    args = [turned, before, *orders, *pieces]
    shapes = [jax.ShapeDtypeStruct((cols, 2 * q_rows // parts), F32)] * parts
    return pl.pallas_call(
        functools.partial(late_kernel, len(pieces), first),
        in_specs=[IN_VMEM] * len(args),
        out_specs=[IN_VMEM] * parts,
        out_shape=shapes,
        compiler_params=SMALL,
        cost_estimate=FREE,
        name="late_scores",
    )(*args)


def reduce_kernel(parts, crossing, seqs, sets, *refs):
    own, other = refs[-2:]
    rows = own.shape[1]
    where = {key: (g, n) for g, keys in enumerate(sets) for n, key in enumerate(keys)}
    for k in range(parts):
        for e in range(crossing):
            total = None
            for m in range(parts):
                g, n = where[k ^ m, e]
                got = refs[g * parts + m][pl.ds(n * seqs, seqs), :]
                total = got if total is None else total + got
            place = pl.ds((k * crossing + e) * seqs, seqs)
            own[place, :] = total[:, :rows]
            other[place, :] = total[:, rows:]


def reduce(parts, crossing, seqs, sets, messages):
    flat = [message for group in messages for message in group]
    shape = jax.ShapeDtypeStruct((parts * crossing * seqs, flat[0].shape[1] // 2), F32)
    return pl.pallas_call(
        functools.partial(reduce_kernel, parts, crossing, seqs, sets),
        in_specs=[IN_VMEM] * len(flat),
        out_specs=[IN_VMEM] * 2,
        out_shape=[shape] * 2,
        compiler_params=PARAMS,
        cost_estimate=FREE,
        name="reduce",
    )(*flat)


def finish_kernel(parts, dp, seqs, own, other, out, columns):
    z, d = lax.axis_index("feat"), lax.axis_index("dp")
    crossed = (0, dp // 2)
    for k in range(parts):
        for n, e in enumerate(crossed):
            for flip, ref in ((0, own), (1, other)):
                place = ((d ^ e ^ flip) * parts + (z ^ k)) * seqs
                rows = ref[pl.ds((k * len(crossed) + n) * seqs, seqs), :]
                columns[pl.ds(pl.multiple_of(place, seqs), seqs), :] = rows
    out[...] = columns[...].T


def finish(parts, dp, seqs, own, other):
    rows = own.shape[1]
    total = parts * dp * seqs
    return pl.pallas_call(
        functools.partial(finish_kernel, parts, dp, seqs),
        in_specs=[IN_VMEM] * 2,
        out_specs=IN_VMEM,
        out_shape=jax.ShapeDtypeStruct((rows, total), F32),
        scratch_shapes=[pltpu.VMEM((total, rows), F32)],
        compiler_params=PARAMS,
        cost_estimate=FREE,
        name="finish",
    )(own, other)


def swap(array, axis, size, by):
    return lax.ppermute(array, axis, [(i, i ^ by) for i in range(size)])


def after(array, *earlier):
    return lax.optimization_barrier((array, *earlier))[0]


def direct(parts, dp, layer_in, grad_out, in_proj, out_proj, queries, seq_ids, valid_counts, owner_order):
    seqs = valid_counts.shape[0]
    span = in_proj.shape[1] // parts
    cut = span * SPLIT // 8
    me = lax.axis_index("feat")
    cross = lambda array: swap(array, "dp", dp, dp // 2)
    pair = lambda array: swap(array, "dp", dp, 1)
    move = lambda array, k: swap(array, "feat", parts, k)
    order = jnp.take(owner_order.reshape(parts, -1), me ^ jnp.arange(parts), axis=0).reshape(1, -1)
    orders = [order, pair(order)]
    low, (g2, g1) = project(
        parts, [(2, 0, span, False), (1, 0, span, False)], layer_in, grad_out, in_proj, out_proj, seq_ids, valid_counts
    )
    g0, g3a, g3b = grads(parts, [(0, 0, span, False), (3, 0, cut, False), (3, cut, span - cut, True)], *low)
    both = [queries, pair(after(queries, g1))]
    x0 = cross(g0)
    z1 = move(g1, 1)
    z2 = move(g2, 2)
    z3a = move(after(g3a, z1), 3)
    x1p = cross(g1)
    x1 = move(after(x1p, z1), 1)
    near, turned = near_scores(parts, both, orders, [g0, x0, z1, z2])
    z3b = move(after(g3b, z1), 3)
    x2 = cross(z2)
    x3a = cross(after(z3a, near[0]))
    x3b = cross(z3b)
    sent = [near[0]] + [move(near[m], m) for m in range(1, parts)]
    part = part_scores(turned, [x1, x2, z3a, x3a])
    far = late_scores(parts, cut, turned, part, orders, [x1, x2, z3b, x3b])
    messages = [sent, [far[0]] + [move(far[m], m) for m in range(1, parts)]]
    sets = [[(0, 0), (0, 1), (1, 0), (2, 0)], [(1, 1), (2, 1), (3, 0), (3, 1)]]
    own, other = reduce(parts, 2, seqs, sets, messages)
    return finish(parts, dp, seqs, own, pair(other))


def gathered(parts, dp, layer_in, grad_out, in_proj, out_proj, queries, seq_ids, valid_counts, owner_order):
    span = in_proj.shape[1] // parts
    ask = [(k, 0, span, False) for k in range(parts)]
    _, own = project(parts, ask, layer_in, grad_out, in_proj, out_proj, seq_ids, valid_counts)
    own = jnp.stack(own)
    own = jnp.take(own, lax.axis_index("feat") ^ jnp.arange(parts), axis=0)
    size = own.shape[1]
    rows = lax.all_to_all(own, "feat", split_axis=0, concat_axis=0, tiled=True)
    rows = lax.all_gather(rows, "dp", axis=0, tiled=True)
    q_rows = queries.shape[0]
    by_row = queries.reshape(q_rows, size, -1)
    scored = jnp.einsum("qij,gisj->qgs", by_row, rows, preferred_element_type=F32)
    scored = jnp.take(scored.reshape(q_rows, -1), owner_order % q_rows, axis=0)
    return lax.psum_scatter(scored, "feat", scatter_dimension=0, tiled=True)


def solution(mesh):
    parts, dp = mesh.shape["feat"], mesh.shape["dp"]
    in_specs = (
        P(("dom", "dp", "feat"), None),
        P(("dom", "dp", "feat"), None),
        P(),
        P(),
        P(("dom", "dp"), "feat"),
        P(("dom", "dp", "feat"), None),
        P(("dom", "dp", "feat")),
        P(("dom", "dp")),
    )
    out_specs = P(("dom", "dp", "feat"), None)
    body = functools.partial(direct if parts == 4 and dp == 4 else gathered, parts, dp)
    return jax.shard_map(body, mesh=mesh, in_specs=in_specs, out_specs=out_specs, check_vma=False)
```
